256 devices in a mesh: teacher: 4 (over y), dp: 16 (over x, z_lo, core), tensor: 4 (over z_hi).
Axes of the slice: x: 4, y: 4, z: 8 (z_hi: 4, z_lo: 2; z = z_hi * 2 + z_lo), core: 2. Of those that a mesh axis runs over, the one named last changes fastest.
Arguments:
- teacher_inputs: bfloat16 [131072, 6144], P(('teacher', 'dp'), 'tensor'), may hold values from -6 to 6
- teacher_keys: bfloat16 [131072, 1024], P(('teacher', 'dp', 'tensor')), may hold values from -6 to 6
- w_key: bfloat16 [1024, 6144], P(('teacher', 'dp'), 'tensor'), may hold values from -0.109375 to 0.109375
- mask_key: int32 [1024, 1536], P(('teacher', 'dp'), 'tensor'), may hold values from 0 to 5
Outputs:
- grad_key: float32 [1024, 6144], P(('teacher', 'dp'), 'tensor')
The draws below stay inside these ranges and needn't reach their ends.
Inputs may be any that keep to these rules, and one draw needn't show every extreme that they name: `mask_key`: each entry names which two of the four weights of its group along 6144 are kept: 0 keeps positions (0,1), 1 (0,2), 2 (0,3), 3 (1,2), 4 (1,3), 5 (2,3).
All inputs are finite; a program needn't handle non-finite values.
Results may differ from the reference program's by a relative error of at most 0.0011.
Values may be sent and summed in bfloat16 or wider, within the bound.
A program may use at most 192 MiB of HBM per device.

```python
import jax
import jax.numpy as jnp
from jax import lax

D = 6144
KV = 1024
ROWS_G = 2048
TOKENS = 131072
N_TEACHER = 4
N_DP = 16
N_TENSOR = 4


def plant(entries, stream_key, low, high):
    longest = entries.shape.index(max(entries.shape))
    spots = []
    for shift in (0, 1):
        where = [jax.random.randint(jax.random.fold_in(stream_key, axis), (), 0, length) for axis, length in enumerate(entries.shape)]
        where[longest] = (where[longest] + shift) % entries.shape[longest]
        spots.append(tuple(where))
    return entries.at[spots[0]].set(low).at[spots[1]].set(high)


def level_of(own_key, dims, split, least, top_value):
    loudness, own = 1.0, jax.random.fold_in(own_key, 6)
    for dim, blocks in split:
        heights = jnp.exp(jax.random.uniform(jax.random.fold_in(own, dim), (blocks,), jnp.float32, least / len(split), top_value / len(split)))
        loudness = loudness * jnp.repeat(heights, dims[dim] // blocks).reshape([-1 if axis == dim else 1 for axis in range(len(dims))])
    return loudness


def bell_draw(own_key, dims, deviation, limit, shards=(), dtype=jnp.bfloat16):
    entries = deviation * jax.random.normal(own_key, dims, jnp.float32)
    if shards:
        entries = entries * level_of(own_key, dims, shards, -0.22, 0.18)
    return jnp.clip(entries, -limit, limit).astype(dtype)


def setup_inputs(seed: int = 0) -> dict:
    keys = jax.random.split(jax.random.key(seed), 5)
    return {
        "teacher_inputs": bell_draw(keys[0], (TOKENS, D), 1.0, 6.0, ((0, 64), (1, 4))),
        "teacher_keys": bell_draw(keys[1], (TOKENS, KV), 1.0, 6.0, ((0, 256),)),
        "w_key": bell_draw(keys[2], (KV, D), (D // 2) ** -0.5, 0.109375, ((0, 64), (1, 4))),
        "mask_key": plant(jax.random.randint(keys[3], (KV, D // 4), 0, 6), jax.random.fold_in(keys[3], 1), 0, 5).astype(jnp.int32),
    }


def kept_pair(pattern):
    upper = (pattern >= 3).astype(jnp.int32)
    last = (pattern >= 5).astype(jnp.int32)
    low_pos = upper + last
    high_pos = pattern + 1 - 2 * upper - last
    return [((low_pos == j) | (high_pos == j)).astype(jnp.float32) for j in range(4)]


def expand_last(pattern):
    return jnp.stack(kept_pair(pattern), axis=-1).reshape(pattern.shape[0], -1)


def reference(teacher_inputs, teacher_keys, w_key, mask_key):
    kept_mask = expand_last(mask_key)
    masked = w_key * kept_mask.astype(jnp.bfloat16)
    quarter = D // N_TENSOR
    loss_scale = 1.0 / (TOKENS ** 0.5)
    groups = N_TEACHER * N_DP
    input_groups = teacher_inputs.reshape(groups, ROWS_G, D)
    target_groups = teacher_keys.reshape(groups, ROWS_G, KV)

    def one_group(running, pair):
        inputs, targets = pair
        outputs = jnp.zeros((ROWS_G, KV), jnp.float32)
        for column in range(N_TENSOR):
            partial_value = jnp.dot(inputs[:, column * quarter:(column + 1) * quarter],
                              masked[:, column * quarter:(column + 1) * quarter].T,
                              preferred_element_type=jnp.float32)
            outputs = outputs + lax.optimization_barrier(partial_value.astype(jnp.bfloat16)).astype(jnp.float32)
        signal = ((outputs - targets.astype(jnp.float32)) * loss_scale).astype(jnp.bfloat16)
        grad_term = lax.dot_general(signal, inputs, (((0,), (0,)), ((), ())), preferred_element_type=jnp.float32)
        rounded = lax.optimization_barrier(grad_term.astype(jnp.bfloat16))
        return running + rounded.astype(jnp.float32), None

    summed, unused = lax.scan(one_group, jnp.zeros((KV, D), jnp.float32), (input_groups, target_groups))
    return kept_mask * summed
```

```python
import functools
import math

import jax
import jax.numpy as jnp
from jax import lax
from jax.experimental import pallas as pl
from jax.experimental.pallas import tpu as pltpu
from jax.sharding import PartitionSpec as P

MESH = pl.DeviceIdType.MESH
F32 = jnp.float32
BF16 = jnp.bfloat16
PIECES = 4


def pair(core, t):
    return (1 - core) * (t + 1 - 2 * lax.rem(t, 2)) + core * (3 - t)


def device(y, x, l, c, t):
    return {"teacher": y, "dp": x * 4 + l * 2 + c, "tensor": t}


def kept_of(mask_ref, quarter):
    rows, groups = mask_ref.shape
    pattern = mask_ref[...].astype(F32).astype(BF16)
    spread_row = lax.broadcasted_iota(jnp.int32, (128, 512), 0)
    spread_col = lax.broadcasted_iota(jnp.int32, (128, 512), 1)
    spread = jnp.where(spread_col // 4 == spread_row, 1.0, 0.0).astype(BF16)
    place = (lax.broadcasted_iota(jnp.int32, (rows, 512), 1) % 4).astype(F32)
    parts = []
    for i in range(groups // 128):
        p = jnp.dot(pattern[:, i * 128:(i + 1) * 128], spread, preferred_element_type=F32)
        upper = jnp.where(p > 2.5, 1.0, 0.0)
        last = jnp.where(p > 4.5, 1.0, 0.0)
        low = upper + last
        high = p + 1.0 - 2.0 * upper - last
        parts.append(jnp.where((low == place) | (high == place), 1.0, 0.0))
    return jnp.concatenate(parts, axis=1)


def kernel(scale, x_ref, y_ref, w_ref, mask_ref, o_ref,
           xb, wb, yt, ptf, pb, pr, sb, gb, ar, bs, br, zs, fr, kept, masked,
           x_send, x_recv, x_own, w0_send, w0_recv, wa_send, wa_recv, wb_send, wb_recv,
           p_send, p_recv, a_send, a_recv, b_send, b_recv, f_send, f_recv):
    y = lax.axis_index("teacher")
    d = lax.axis_index("dp")
    t = lax.axis_index("tensor")
    x = lax.div(d, 4)
    l = lax.rem(lax.div(d, 2), 2)
    c = lax.rem(d, 2)
    a = x + c * (y - x)
    b = y + c * (x - y)
    q = pair(c, t)
    u = pair(1 - c, t)
    block_rows, quarter = xb.shape[1], xb.shape[2] // 2
    piece = 2 * quarter // PIECES
    chunk = wb.shape[1] * wb.shape[2]

    def along_a(n):
        other = lax.rem(a + n, 4)
        return other, device(y + c * (other - y), x + (1 - c) * (other - x), l, c, t)

    def along_b(n):
        other = lax.rem(b + n, 4)
        return other, device(y + (1 - c) * (other - y), x + c * (other - x), l, c, t)

    def owner(e):
        return lax.rem(l + lax.div(e, 2), 2), lax.rem(c + lax.rem(e, 2), 2)

    def send(src, dst, ss, rs, to):
        return pltpu.make_async_remote_copy(
            src_ref=src, dst_ref=dst, send_sem=ss, recv_sem=rs, device_id=to, device_id_type=MESH)

    barrier = pltpu.get_barrier_semaphore()
    friends = [along_a(n)[1] for n in (1, 2, 3)] + [along_b(n)[1] for n in (1, 2, 3)]
    friends += [device(y, x, l, c, u)]
    for e in range(4):
        le, ce = owner(jnp.int32(e))
        if e:
            friends.append(device(y, x, le, ce, t))
        friends.append(device(y, x, le, ce, q))
        if e % 2:
            friends.append(device(y, x, le, ce, u))
    for friend in friends:
        pl.semaphore_signal(barrier, 1, device_id=friend, device_id_type=MESH)

    own_copies = []
    for slot, block in ((0, t), (1, u)):
        own_copies.append(pltpu.make_async_copy(
            x_ref.at[pl.ds(block * block_rows, block_rows)], xb.at[slot, :, pl.ds(0, quarter)], x_own.at[slot]))
    kept[...] = kept_of(mask_ref, quarter)
    masked[...] = (w_ref[...].astype(F32) * kept[...]).astype(BF16)
    wb[l * 2 + c, b * 4 + a, :, pl.ds(0, quarter)] = masked[...]

    pl.semaphore_wait(barrier, len(friends))

    w0 = []
    for e in range(4):
        le, ce = owner(jnp.int32(e))
        spot = (y + ce * (x - y)) * 4 + x + ce * (y - x)
        if e:
            w0.append(send(masked, wb.at[l * 2 + c, spot, :, pl.ds(0, quarter)],
                           w0_send.at[0, e], w0_recv.at[0, e], device(y, x, le, ce, t)))
        w0.append(send(masked, wb.at[l * 2 + c, spot, :, pl.ds(quarter, quarter)],
                       w0_send.at[1, e], w0_recv.at[1, e], device(y, x, le, ce, pair(ce, t))))
    for copy in w0:
        copy.start()

    swaps = []
    for slot, block in ((0, q), (1, pair(1 - c, q))):
        swaps.append(send(x_ref.at[pl.ds(block * block_rows, block_rows)], xb.at[slot, :, pl.ds(quarter, quarter)],
                          x_send.at[slot], x_recv.at[slot], device(y, x, l, c, q)))
    for copy in swaps:
        copy.start()
    for copy in own_copies:
        copy.start()

    for copy in w0:
        copy.wait_recv()
    wa = []
    for n in (1, 2, 3):
        wa.append(send(wb.at[:, b * 4 + a], wb.at[:, b * 4 + a], wa_send.at[n - 1], wa_recv.at[n - 1], along_a(n)[1]))
    for copy in wa:
        copy.start()
    for copy in wa:
        copy.wait_recv()
    wg = []
    for n in (1, 2, 3):
        wg.append(send(wb.at[:, pl.ds(b * 4, 4)], wb.at[:, pl.ds(b * 4, 4)],
                       wb_send.at[n - 1], wb_recv.at[n - 1], along_b(n)[1]))
    for copy in wg:
        copy.start()

    def targets(e, carry):
        le, ce = owner(e)
        row = lax.broadcasted_iota(jnp.int32, (chunk, 1), 0)
        row_b, row_a, row_r = row // 64, (row // 16) % 4, row % 16
        key = (row_b + c * (row_a - row_b)) * 256 + (row_a + c * (row_b - row_a)) * 64 + le * 32 + ce * 16 + row_r
        column = lax.broadcasted_iota(jnp.int32, (chunk, y_ref.shape[1]), 1)
        choose = jnp.where(column == key, 1.0, 0.0).astype(BF16)
        yt[e] = lax.dot_general(choose, y_ref[...], (((1,), (1,)), ((), ())),
                                preferred_element_type=F32).astype(BF16)
        return carry

    lax.fori_loop(0, 4, targets, 0)

    for copy in own_copies:
        copy.wait()
    for copy in wg:
        copy.wait_recv()
    for copy in swaps:
        copy.wait_recv()

    def partial_copy(e, slot):
        return send(pb.at[e, slot], pr.at[e, 1 - slot], p_send.at[e, slot], p_recv.at[e, 1 - slot],
                    device(y, x, l, c, u))

    def partials(k, carry):
        e = 3 - k
        le, ce = owner(e)
        rows = wb[le * 2 + ce].reshape(chunk, 2 * quarter)
        for slot in range(2):
            part = lax.dot_general(rows, xb[slot], (((1,), (1,)), ((), ())), preferred_element_type=F32)
            if slot == 0:
                part = part - yt[e].astype(F32)
            ptf[e, slot] = part
            pb[e, slot] = part.astype(BF16)
            partial_copy(e, slot).start()
        return carry

    lax.fori_loop(0, 4, partials, 0)

    def a_copy(e, i, n):
        other, to = along_a(n)
        return send(gb.at[e, :, other, :, pl.ds(i * piece, piece)], ar.at[e, n - 1, :, :, pl.ds(i * piece, piece)],
                    a_send.at[e], a_recv.at[e, i, n - 1], to)

    def b_copy(e, i, n):
        other, to = along_b(n)
        return send(bs.at[e, other, :, pl.ds(i * piece, piece)], br.at[e, n - 1, :, pl.ds(i * piece, piece)],
                    b_send.at[e], b_recv.at[e, i, n - 1], to)

    def f_copy(e, slot):
        le, ce = owner(e)
        return send(zs.at[e, :, pl.ds(slot * quarter, quarter)], fr.at[slot, e],
                    f_send.at[slot, e], f_recv.at[slot, e], device(y, x, le, ce, q if slot else t))

    def gradient(e):
        for slot in range(2):
            partial_copy(e, 1 - slot).wait_recv()
            total = ptf[e, slot] + pr[e, slot].astype(F32)
            sb[:, slot * block_rows:(slot + 1) * block_rows] = (total * scale).astype(BF16)
        for i in range(PIECES):
            rows = xb[:, :, i * piece:(i + 1) * piece].reshape(2 * block_rows, piece)
            term = jnp.dot(sb[...], rows, preferred_element_type=F32)
            gb[e, :, :, :, i * piece:(i + 1) * piece] = term.astype(BF16).reshape(4, 4, 16, piece)
            for n in (1, 2, 3):
                a_copy(e, i, n).start()

    def reduce_a(e):
        for i in range(PIECES):
            cols = slice(i * piece, (i + 1) * piece)
            for n in (1, 2, 3):
                a_copy(e, i, n).wait_recv()
            total = gb[e, :, a, :, cols].astype(F32)
            for n in range(3):
                total = total + ar[e, n, :, :, cols].astype(F32)
            bs[e, :, :, cols] = total.astype(BF16)
            for n in (1, 2, 3):
                b_copy(e, i, n).start()

    def reduce_b(e):
        for i in range(PIECES):
            cols = slice(i * piece, (i + 1) * piece)
            for n in (1, 2, 3):
                b_copy(e, i, n).wait_recv()
            total = bs[e, b, :, cols].astype(F32)
            for n in range(3):
                total = total + br[e, n, :, cols].astype(F32)
            zs[e, :, cols] = total
        f_copy(e, 1).start()

        @pl.when(e > 0)
        def _():
            f_copy(e, 0).start()

    def steps(k, carry):
        @pl.when(k < 4)
        def _():
            gradient(3 - k)

        @pl.when((k >= 1) & (k < 5))
        def _():
            reduce_a(4 - k)

        @pl.when(k >= 2)
        def _():
            reduce_b(5 - k)

        return carry

    lax.fori_loop(0, 6, steps, 0)

    total = zs[0, :, 0:quarter]
    for e in range(4):
        if e:
            f_copy(jnp.int32(e), 0).wait_recv()
            total = total + fr[0, e]
        f_copy(jnp.int32(e), 1).wait_recv()
        total = total + fr[1, e]
    o_ref[...] = kept[...] * total

    for copy in w0 + swaps + wa + wg:
        copy.wait_send()

    def drain(e, carry):
        for slot in range(2):
            partial_copy(e, slot).wait_send()
        pltpu.make_async_copy(ar.at[e], ar.at[e], a_send.at[e]).wait()
        pltpu.make_async_copy(br.at[e], br.at[e], b_send.at[e]).wait()
        f_copy(e, 1).wait_send()

        @pl.when(e > 0)
        def _():
            f_copy(e, 0).wait_send()

        return carry

    lax.fori_loop(0, 4, drain, 0)


def body(teacher_inputs, teacher_keys, w_key, mask_key):
    rows, quarter = teacher_inputs.shape
    block_rows, keys = teacher_keys.shape
    groups = lax.axis_size("teacher") * lax.axis_size("dp")
    scale = 1.0 / math.sqrt(rows * groups)
    width = 2 * quarter
    dma = pltpu.SemaphoreType.DMA
    vmem = pl.BlockSpec(memory_space=pltpu.VMEM)
    return pl.pallas_call(
        functools.partial(kernel, scale),
        out_shape=jax.ShapeDtypeStruct((16, quarter), F32),
        in_specs=[pl.BlockSpec(memory_space=pl.ANY), vmem, vmem, vmem],
        out_specs=vmem,
        scratch_shapes=[
            pltpu.VMEM((2, block_rows, width), BF16),
            pltpu.VMEM((4, 16, 16, width), BF16),
            pltpu.VMEM((4, keys // 4, block_rows), BF16),
            pltpu.VMEM((4, 2, keys // 4, block_rows), F32),
            pltpu.VMEM((4, 2, keys // 4, block_rows), BF16),
            pltpu.VMEM((4, 2, keys // 4, block_rows), BF16),
            pltpu.VMEM((keys // 4, 2 * block_rows), BF16),
            pltpu.VMEM((4, 4, 4, 16, width), BF16),
            pltpu.VMEM((4, 3, 4, 16, width), BF16),
            pltpu.VMEM((4, 4, 16, width), BF16),
            pltpu.VMEM((4, 3, 16, width), BF16),
            pltpu.VMEM((4, 16, width), F32),
            pltpu.VMEM((2, 4, 16, quarter), F32),
            pltpu.VMEM((16, quarter), F32),
            pltpu.VMEM((16, quarter), BF16),
            dma((2,)), dma((2,)), dma((2,)),
            dma((2, 4)), dma((2, 4)),
            dma((3,)), dma((3,)), dma((3,)), dma((3,)),
            dma((4, 2)), dma((4, 2)),
            dma((4,)), dma((4, PIECES, 3)),
            dma((4,)), dma((4, PIECES, 3)),
            dma((2, 4)), dma((2, 4)),
        ],
        compiler_params=pltpu.CompilerParams(
            collective_id=0, has_side_effects=True, vmem_limit_bytes=60 * 2**20),
    )(teacher_inputs, teacher_keys, w_key, mask_key)


def solution(mesh):
    placed = (
        P(("teacher", "dp"), "tensor"),
        P(("teacher", "dp", "tensor"), None),
        P(("teacher", "dp"), "tensor"),
        P(("teacher", "dp"), "tensor"),
    )
    return jax.shard_map(
        body, mesh=mesh, in_specs=placed, out_specs=P(("teacher", "dp"), "tensor"), check_vma=False
    )
```

```python
import functools
import math

import jax
import jax.numpy as jnp
from jax import lax
from jax.experimental import pallas as pl
from jax.experimental.pallas import tpu as pltpu
from jax.sharding import PartitionSpec as P

MESH = pl.DeviceIdType.MESH
F32 = jnp.float32
BF16 = jnp.bfloat16
GROUPS = 128
BLOCK = 4 * GROUPS
PIECES = 3


def pair(core, t):
    return (1 - core) * (t + 1 - 2 * lax.rem(t, 2)) + core * (3 - t)


def device(y, x, l, c, t):
    return {"teacher": y, "dp": x * 4 + l * 2 + c, "tensor": t}


def spread_matrix():
    row = lax.broadcasted_iota(jnp.int32, (GROUPS, BLOCK), 0)
    column = lax.broadcasted_iota(jnp.int32, (GROUPS, BLOCK), 1)
    return jnp.where(column // 4 == row, 1.0, 0.0).astype(BF16)


def squeeze_matrix():
    row = lax.broadcasted_iota(jnp.int32, (BLOCK, GROUPS), 0)
    column = lax.broadcasted_iota(jnp.int32, (BLOCK, GROUPS), 1)
    return jnp.where(row // 4 == column, 1.0, 0.0).astype(BF16)


def kept_places(pattern, spread):
    p = jnp.dot(pattern, spread, preferred_element_type=F32)
    place = (lax.broadcasted_iota(jnp.int32, p.shape, 1) % 4).astype(F32)
    upper = jnp.where(p > 2.5, 1.0, 0.0)
    last = jnp.where(p > 4.5, 1.0, 0.0)
    return upper + last == place, p + 1.0 - 2.0 * upper - last == place


def spread_exactly(values, spread):
    total = None
    for _ in range(3):
        part = values.astype(BF16)
        values = values - part.astype(F32)
        wide = jnp.dot(part, spread, preferred_element_type=F32)
        total = wide if total is None else total + wide
    return total


def kernel(scale, x_ref, y_ref, w_ref, mask_ref, o_ref,
           xb, yb, wc, wb, ml, mh, yt, ptf, pb, pr, sb, gb, ah, ar, bs, bh, br, zs, fr, own,
           x_send, x_recv, x_own, y_own, w0_send, w0_recv, wa_send, wa_recv, wb_send, wb_recv,
           p_send, p_recv, a1_send, a1_recv, a2_send, a2_recv, b1_send, b1_recv, b2_send, b2_recv, f_send, f_recv):
    y = lax.axis_index("teacher")
    d = lax.axis_index("dp")
    t = lax.axis_index("tensor")
    x = lax.div(d, 4)
    l = lax.rem(lax.div(d, 2), 2)
    c = lax.rem(d, 2)
    a = x + c * (y - x)
    b = y + c * (x - y)
    q = pair(c, t)
    u = pair(1 - c, t)
    block_rows, quarter = xb.shape[1], xb.shape[2] // 2
    blocks = quarter // BLOCK
    third = quarter // 4
    packed = 3 * third
    half_width = quarter // 2
    piece = quarter // PIECES
    chunk = wb.shape[1]

    def along_a(n):
        other = lax.rem(a + n, 4)
        return other, device(y + c * (other - y), x + (1 - c) * (other - x), l, c, t)

    def along_b(n):
        other = lax.rem(b + n, 4)
        return other, device(y + (1 - c) * (other - y), x + c * (other - x), l, c, t)

    def owner(e):
        return lax.rem(l + lax.div(e, 2), 2), lax.rem(c + lax.rem(e, 2), 2)

    def send(src, dst, ss, rs, to):
        return pltpu.make_async_remote_copy(
            src_ref=src, dst_ref=dst, send_sem=ss, recv_sem=rs, device_id=to, device_id_type=MESH)

    barrier = pltpu.get_barrier_semaphore()
    friends = [along_a(n)[1] for n in (1, 2, 3)] + [along_b(n)[1] for n in (1, 2, 3)]
    friends += [device(y, x, l, c, u)]
    for e in range(4):
        le, ce = owner(jnp.int32(e))
        if e:
            friends.append(device(y, x, le, ce, t))
        friends.append(device(y, x, le, ce, q))
        if e % 2:
            friends.append(device(y, x, le, ce, u))
    for friend in friends:
        pl.semaphore_signal(barrier, 1, device_id=friend, device_id_type=MESH)

    own_copies = []
    for slot, block in ((0, t), (1, u)):
        own_copies.append(pltpu.make_async_copy(
            x_ref.at[pl.ds(block * block_rows, block_rows)], xb.at[slot, :, pl.ds(0, quarter)], x_own.at[slot]))
    spread, squeeze = spread_matrix(), squeeze_matrix()
    own[:, 2 * third:] = mask_ref[...].astype(F32).astype(BF16)
    for i in range(blocks):
        low, high = kept_places(own[:, 2 * third + i * GROUPS:2 * third + (i + 1) * GROUPS], spread)
        weights = w_ref[:, i * BLOCK:(i + 1) * BLOCK].astype(F32)
        for side, place in enumerate((low, high)):
            own[:, side * third + i * GROUPS:side * third + (i + 1) * GROUPS] = jnp.dot(
                jnp.where(place, weights, 0.0).astype(BF16), squeeze, preferred_element_type=F32).astype(BF16)
    wc[l * 2 + c, b * 4 + a, :, pl.ds(0, packed)] = own[...]

    pl.semaphore_wait(barrier, len(friends))

    w0 = []
    for e in range(4):
        le, ce = owner(jnp.int32(e))
        spot = (y + ce * (x - y)) * 4 + x + ce * (y - x)
        if e:
            w0.append(send(own, wc.at[l * 2 + c, spot, :, pl.ds(0, packed)],
                           w0_send.at[0, e], w0_recv.at[0, e], device(y, x, le, ce, t)))
        w0.append(send(own, wc.at[l * 2 + c, spot, :, pl.ds(packed, packed)],
                       w0_send.at[1, e], w0_recv.at[1, e], device(y, x, le, ce, pair(ce, t))))
    for copy in w0:
        copy.start()

    swaps = []
    for slot, block in ((0, q), (1, pair(1 - c, q))):
        swaps.append(send(x_ref.at[pl.ds(block * block_rows, block_rows)], xb.at[slot, :, pl.ds(quarter, quarter)],
                          x_send.at[slot], x_recv.at[slot], device(y, x, l, c, q)))
    for copy in own_copies:
        copy.start()
    y_copy = pltpu.make_async_copy(y_ref, yb, y_own)
    y_copy.start()

    def to_both(part, ss, rs, along):
        copies = [send(part(0, slice(None)), part(0, slice(None)), ss.at[i], rs.at[i], along(n)[1])
                  for i, n in ((0, 1), (1, 3))]
        for copy in copies:
            copy.start()
        return copies

    def pass_on(part, ss, rs, along):
        copies = [send(part(back, half), part(back, half), ss.at[i], rs.at[i], along(n)[1])
                  for i, n, back, half in ((2, 1, 3, slice(0, 2)), (3, 3, 1, slice(2, 4)))]
        for copy in copies:
            copy.start()
        return copies

    def part_a(n, half):
        return wc.at[half, b * 4 + lax.rem(a + n, 4)]

    def part_b(n, half):
        return wc.at[half, pl.ds(lax.rem(b + n, 4) * 4, 4)]

    for copy in w0:
        copy.wait_recv()
    for copy in swaps:
        copy.start()
    gathers = []
    for part, ss, rs, along in ((part_a, wa_send, wa_recv, along_a), (part_b, wb_send, wb_recv, along_b)):
        first = to_both(part, ss, rs, along)
        for copy in first:
            copy.wait_recv()
        second = pass_on(part, ss, rs, along)
        if part is part_a:
            for copy in second:
                copy.wait_recv()
        gathers += first + second

    def targets(e, carry):
        le, ce = owner(e)
        row = lax.broadcasted_iota(jnp.int32, (chunk, 1), 0)
        row_b, row_a, row_r = row // 64, (row // 16) % 4, row % 16
        key = (row_b + c * (row_a - row_b)) * 256 + (row_a + c * (row_b - row_a)) * 64 + le * 32 + ce * 16 + row_r
        column = lax.broadcasted_iota(jnp.int32, (chunk, yb.shape[1]), 1)
        choose = jnp.where(column == key, 1.0, 0.0).astype(BF16)
        yt[e] = lax.dot_general(choose, yb[...], (((1,), (1,)), ((), ())),
                                preferred_element_type=F32).astype(BF16)
        return carry

    y_copy.wait()
    lax.fori_loop(0, 4, targets, 0)

    for copy in own_copies:
        copy.wait()
    for copy in second:
        copy.wait_recv()

    def unpack(j, carry):
        for i in range(2 * blocks):
            base = i // blocks * packed + i % blocks * GROUPS
            cols = slice(i * BLOCK, (i + 1) * BLOCK)
            parts = [wc[j, :, :, base + side * third:base + side * third + GROUPS].reshape(chunk, GROUPS)
                     for side in range(3)]
            low, high = kept_places(parts[2], spread)
            wide = [jnp.dot(part, spread, preferred_element_type=F32) for part in parts[:2]]
            wb[j, :, cols] = jnp.where(low, wide[0], jnp.where(high, wide[1], 0.0)).astype(BF16)
            ml[j, :, cols] = jnp.where(low, 1.0, 0.0).astype(BF16)
            mh[j, :, cols] = jnp.where(high, 1.0, 0.0).astype(BF16)
        return carry

    lax.fori_loop(0, 4, unpack, 0)
    swaps[0].wait_recv()

    def partial_copy(e, slot):
        return send(pb.at[e, slot], pr.at[e, 1 - slot], p_send.at[e, slot], p_recv.at[e, 1 - slot],
                    device(y, x, l, c, u))

    def partials(k, carry):
        e = 3 - k
        le, ce = owner(e)
        rows = wb[le * 2 + ce]
        for slot in range(2):
            if slot == 1:
                @pl.when(k == 0)
                def _():
                    swaps[1].wait_recv()
            part = lax.dot_general(rows, xb[slot], (((1,), (1,)), ((), ())), preferred_element_type=F32)
            if slot == 0:
                part = part - yt[e].astype(F32)
            ptf[e, slot] = part
            pb[e, slot] = part.astype(BF16)
            partial_copy(e, slot).start()
        return carry

    lax.fori_loop(0, 4, partials, 0)

    def cols_of(i):
        return pl.ds(i * piece, piece)

    def hand(e, i, side, src, dst, ss, rs, along):
        return send(src, dst.at[e, side, :, :, cols_of(i)] if len(dst.shape) == 5 else dst.at[e, side, :, cols_of(i)],
                    ss.at[e], rs.at[e, i, side], along(1 + 2 * side)[1])

    def a_far(e, i, side):
        return hand(e, i, side, gb.at[e, pl.ds(2 * side, 2), lax.rem(a + 2, 4), :, cols_of(i)],
                    ah, a1_send, a1_recv, along_a)

    def a_near(e, i, side):
        return hand(e, i, side, gb.at[e, :, lax.rem(a + 1 + 2 * side, 4), :, cols_of(i)],
                    ar, a2_send, a2_recv, along_a)

    def b_far(e, i, side):
        return hand(e, i, side, bs.at[e, lax.rem(b + 2, 4), pl.ds(8 * side, 8), cols_of(i)],
                    bh, b1_send, b1_recv, along_b)

    def b_near(e, i, side):
        return hand(e, i, side, bs.at[e, lax.rem(b + 1 + 2 * side, 4), :, cols_of(i)],
                    br, b2_send, b2_recv, along_b)

    def f_copy(e, slot):
        le, ce = owner(e)
        return send(zs.at[e, :, pl.ds(slot * half_width, half_width)], fr.at[slot, e],
                    f_send.at[slot, e], f_recv.at[slot, e], device(y, x, le, ce, q if slot else t))

    def gradient(e):
        for slot in range(2):
            partial_copy(e, 1 - slot).wait_recv()
            total = ptf[e, slot] + pr[e, slot].astype(F32)
            sb[:, slot * block_rows:(slot + 1) * block_rows] = (total * scale).astype(BF16)
        le, ce = owner(e)
        j = le * 2 + ce
        for i in range(PIECES):
            wide = slice(i * 2 * piece, (i + 1) * 2 * piece)
            rows = xb[:, :, wide].reshape(2 * block_rows, 2 * piece)
            term = jnp.dot(sb[...], rows, preferred_element_type=F32).astype(BF16)
            kept = []
            for n in range(2 * piece // BLOCK):
                cols = slice(n * BLOCK, (n + 1) * BLOCK)
                spot = slice(i * 2 * piece + n * BLOCK, i * 2 * piece + (n + 1) * BLOCK)
                for place in (ml, mh):
                    kept.append(jnp.dot(term[:, cols] * place[j, :, spot], squeeze, preferred_element_type=F32))
            gb[e, :, :, :, i * piece:(i + 1) * piece] = (
                jnp.concatenate(kept, axis=1).astype(BF16).reshape(4, 4, 16, piece))
            for side in range(2):
                a_far(e, i, side).start()

    def fold_a(e):
        for i in range(PIECES):
            cols = slice(i * piece, (i + 1) * piece)
            for side in range(2):
                a_far(e, i, side).wait_recv()
                spot = lax.rem(a + 1 + 2 * side, 4)
                half = slice(2 * side, 2 * side + 2)
                gb[e, half, spot, :, cols] = (gb[e, half, spot, :, cols].astype(F32)
                                              + ah[e, side, :, :, cols].astype(F32)).astype(BF16)
                a_near(e, i, side).start()

    def reduce_a(e):
        for i in range(PIECES):
            cols = slice(i * piece, (i + 1) * piece)
            total = gb[e, :, a, :, cols].astype(F32)
            for side in range(2):
                a_near(e, i, side).wait_recv()
                total = total + ar[e, side, :, :, cols].astype(F32)
            bs[e, :, :, cols] = total
            for side in range(2):
                b_far(e, i, side).start()

    def fold_b(e):
        for i in range(PIECES):
            cols = slice(i * piece, (i + 1) * piece)
            for side in range(2):
                b_far(e, i, side).wait_recv()
                spot = lax.rem(b + 1 + 2 * side, 4)
                half = slice(8 * side, 8 * side + 8)
                bs[e, spot, half, cols] = bs[e, spot, half, cols] + bh[e, side, :, cols]
                b_near(e, i, side).start()

    def reduce_b(e):
        for i in range(PIECES):
            cols = slice(i * piece, (i + 1) * piece)
            total = bs[e, b, :, cols]
            for side in range(2):
                b_near(e, i, side).wait_recv()
                total = total + br[e, side, :, cols]
            zs[e, :, cols] = total
        f_copy(e, 1).start()

        @pl.when(e > 0)
        def _():
            f_copy(e, 0).start()

    def steps(k, carry):
        @pl.when(k < 4)
        def _():
            gradient(3 - k)

        @pl.when(k >= 1)
        def _():
            fold_b(4 - k)

        @pl.when(k < 4)
        def _():
            fold_a(3 - k)

        @pl.when(k >= 1)
        def _():
            reduce_b(4 - k)

        @pl.when(k < 4)
        def _():
            reduce_a(3 - k)

        return carry

    lax.fori_loop(0, 5, steps, 0)

    total = zs[0, :, 0:half_width]
    for e in range(4):
        if e:
            f_copy(jnp.int32(e), 0).wait_recv()
            total = total + fr[0, e]
        f_copy(jnp.int32(e), 1).wait_recv()
        total = total + fr[1, e]
    for i in range(blocks):
        low, high = kept_places(own[:, 2 * third + i * GROUPS:2 * third + (i + 1) * GROUPS], spread)
        wide = [spread_exactly(total[:, n * GROUPS:(n + 1) * GROUPS], spread) for n in (2 * i, 2 * i + 1)]
        o_ref[:, i * BLOCK:(i + 1) * BLOCK] = jnp.where(low, wide[0], jnp.where(high, wide[1], 0.0))

    for copy in w0 + swaps + gathers:
        copy.wait_send()

    def drain(e, carry):
        for slot in range(2):
            partial_copy(e, slot).wait_send()
        for landed, sent in ((ah, a1_send), (ar, a2_send), (bh, b1_send), (br, b2_send)):
            pltpu.make_async_copy(landed.at[e], landed.at[e], sent.at[e]).wait()
        f_copy(e, 1).wait_send()

        @pl.when(e > 0)
        def _():
            f_copy(e, 0).wait_send()

        return carry

    lax.fori_loop(0, 4, drain, 0)


def body(teacher_inputs, teacher_keys, w_key, mask_key):
    rows, quarter = teacher_inputs.shape
    block_rows, keys = teacher_keys.shape
    groups = lax.axis_size("teacher") * lax.axis_size("dp")
    scale = 1.0 / math.sqrt(rows * groups)
    width = 2 * quarter
    dma = pltpu.SemaphoreType.DMA
    vmem = pl.BlockSpec(memory_space=pltpu.VMEM)
    return pl.pallas_call(
        functools.partial(kernel, scale),
        out_shape=jax.ShapeDtypeStruct((16, quarter), F32),
        in_specs=[pl.BlockSpec(memory_space=pl.ANY), pl.BlockSpec(memory_space=pl.ANY), vmem, vmem],
        out_specs=vmem,
        scratch_shapes=[
            pltpu.VMEM((2, block_rows, width), BF16),
            pltpu.VMEM((block_rows, keys), BF16),
            pltpu.VMEM((4, 16, 16, 3 * width // 4), BF16),
            pltpu.VMEM((4, keys // 4, width), BF16),
            pltpu.VMEM((4, keys // 4, width), BF16),
            pltpu.VMEM((4, keys // 4, width), BF16),
            pltpu.VMEM((4, keys // 4, block_rows), BF16),
            pltpu.VMEM((4, 2, keys // 4, block_rows), F32),
            pltpu.VMEM((4, 2, keys // 4, block_rows), BF16),
            pltpu.VMEM((4, 2, keys // 4, block_rows), BF16),
            pltpu.VMEM((keys // 4, 2 * block_rows), BF16),
            pltpu.VMEM((4, 4, 4, 16, quarter), BF16),
            pltpu.VMEM((4, 2, 2, 16, quarter), BF16),
            pltpu.VMEM((4, 2, 4, 16, quarter), BF16),
            pltpu.VMEM((4, 4, 16, quarter), F32),
            pltpu.VMEM((4, 2, 8, quarter), F32),
            pltpu.VMEM((4, 2, 16, quarter), F32),
            pltpu.VMEM((4, 16, quarter), F32),
            pltpu.VMEM((2, 4, 16, quarter // 2), F32),
            pltpu.VMEM((16, 3 * quarter // 4), BF16),
            dma((2,)), dma((2,)), dma((2,)), dma(()),
            dma((2, 4)), dma((2, 4)),
            dma((4,)), dma((4,)), dma((4,)), dma((4,)),
            dma((4, 2)), dma((4, 2)),
            dma((4,)), dma((4, PIECES, 2)), dma((4,)), dma((4, PIECES, 2)),
            dma((4,)), dma((4, PIECES, 2)), dma((4,)), dma((4, PIECES, 2)),
            dma((2, 4)), dma((2, 4)),
        ],
        compiler_params=pltpu.CompilerParams(
            collective_id=0, has_side_effects=True, vmem_limit_bytes=60 * 2**20),
    )(teacher_inputs, teacher_keys, w_key, mask_key)


def solution(mesh):
    placed = (
        P(("teacher", "dp"), "tensor"),
        P(("teacher", "dp", "tensor"), None),
        P(("teacher", "dp"), "tensor"),
        P(("teacher", "dp"), "tensor"),
    )
    return jax.shard_map(
        body, mesh=mesh, in_specs=placed, out_specs=P(("teacher", "dp"), "tensor"), check_vma=False
    )
```

```python
import functools
import math

import jax
import jax.numpy as jnp
from jax import lax
from jax.experimental import pallas as pl
from jax.experimental.pallas import tpu as pltpu
from jax.sharding import PartitionSpec as P

MESH = pl.DeviceIdType.MESH
F32 = jnp.float32
BF16 = jnp.bfloat16
GROUPS = 128
BLOCK = 4 * GROUPS
PIECES = 2


def pair(core, t):
    return (1 - core) * (t + 1 - 2 * lax.rem(t, 2)) + core * (3 - t)


def device(y, x, l, c, t):
    return {"teacher": y, "dp": x * 4 + l * 2 + c, "tensor": t}


def spread_matrix():
    row = lax.broadcasted_iota(jnp.int32, (GROUPS, BLOCK), 0)
    column = lax.broadcasted_iota(jnp.int32, (GROUPS, BLOCK), 1)
    return jnp.where(column // 4 == row, 1.0, 0.0).astype(BF16)


def squeeze_matrix():
    row = lax.broadcasted_iota(jnp.int32, (BLOCK, GROUPS), 0)
    column = lax.broadcasted_iota(jnp.int32, (BLOCK, GROUPS), 1)
    return jnp.where(row // 4 == column, 1.0, 0.0).astype(BF16)


def kept_places(pattern, spread):
    p = jnp.dot(pattern, spread, preferred_element_type=F32)
    place = (lax.broadcasted_iota(jnp.int32, p.shape, 1) % 4).astype(F32)
    upper = jnp.where(p > 2.5, 1.0, 0.0)
    last = jnp.where(p > 4.5, 1.0, 0.0)
    return upper + last == place, p + 1.0 - 2.0 * upper - last == place


def spread_exactly(values, spread):
    total = None
    for _ in range(3):
        part = values.astype(BF16)
        values = values - part.astype(F32)
        wide = jnp.dot(part, spread, preferred_element_type=F32)
        total = wide if total is None else total + wide
    return total


def kernel(scale, x_ref, y_ref, w_ref, mask_ref, o_ref,
           xb, yb, wc, wb, ml, mh, yt, ptf, pb, pr, sb, gb, ar, zs, fr, own,
           x_send, x_recv, x_own, y_own, w0_send, w0_recv, wa_send, wa_recv, wb_send, wb_recv,
           p_send, p_recv, a_send, a_recv, f_send, f_recv):
    y = lax.axis_index("teacher")
    d = lax.axis_index("dp")
    t = lax.axis_index("tensor")
    x = lax.div(d, 4)
    l = lax.rem(lax.div(d, 2), 2)
    c = lax.rem(d, 2)
    a = x + c * (y - x)
    b = y + c * (x - y)
    q = pair(c, t)
    u = pair(1 - c, t)
    block_rows, quarter = xb.shape[1], xb.shape[2] // 2
    blocks = quarter // BLOCK
    third = quarter // 4
    packed = 3 * third
    half_width = quarter // 2
    piece = quarter // PIECES
    chunk = wb.shape[1]

    def along_a(n):
        other = lax.rem(a + n, 4)
        return other, device(y + c * (other - y), x + (1 - c) * (other - x), l, c, t)

    def along_b(n):
        other = lax.rem(b + n, 4)
        return other, device(y + (1 - c) * (other - y), x + c * (other - x), l, c, t)

    def across(n):
        other_a, other_b = lax.rem(a + n % 4, 4), lax.rem(b + n // 4, 4)
        to = device(other_b + c * (other_a - other_b), other_a + c * (other_b - other_a), l, c, t)
        return other_b * 4 + other_a, to

    def owner(e):
        return lax.rem(l + lax.div(e, 2), 2), lax.rem(c + lax.rem(e, 2), 2)

    def send(src, dst, ss, rs, to):
        return pltpu.make_async_remote_copy(
            src_ref=src, dst_ref=dst, send_sem=ss, recv_sem=rs, device_id=to, device_id_type=MESH)

    barrier = pltpu.get_barrier_semaphore()
    friends = [across(n)[1] for n in range(1, 16)] + [device(y, x, l, c, u)]
    for e in range(4):
        le, ce = owner(jnp.int32(e))
        if e:
            friends.append(device(y, x, le, ce, t))
        friends.append(device(y, x, le, ce, q))
        if e % 2:
            friends.append(device(y, x, le, ce, u))
    for friend in friends:
        pl.semaphore_signal(barrier, 1, device_id=friend, device_id_type=MESH)

    own_copies = []
    for slot, block in ((0, t), (1, u)):
        own_copies.append(pltpu.make_async_copy(
            x_ref.at[pl.ds(block * block_rows, block_rows)], xb.at[slot, :, pl.ds(0, quarter)], x_own.at[slot]))
    spread, squeeze = spread_matrix(), squeeze_matrix()
    own[:, 2 * third:] = mask_ref[...].astype(F32).astype(BF16)
    for i in range(blocks):
        low, high = kept_places(own[:, 2 * third + i * GROUPS:2 * third + (i + 1) * GROUPS], spread)
        weights = w_ref[:, i * BLOCK:(i + 1) * BLOCK].astype(F32)
        for side, place in enumerate((low, high)):
            own[:, side * third + i * GROUPS:side * third + (i + 1) * GROUPS] = jnp.dot(
                jnp.where(place, weights, 0.0).astype(BF16), squeeze, preferred_element_type=F32).astype(BF16)
    wc[l * 2 + c, b * 4 + a, :, pl.ds(0, packed)] = own[...]

    pl.semaphore_wait(barrier, len(friends))

    w0 = []
    for e in range(4):
        le, ce = owner(jnp.int32(e))
        spot = (y + ce * (x - y)) * 4 + x + ce * (y - x)
        if e:
            w0.append(send(own, wc.at[l * 2 + c, spot, :, pl.ds(0, packed)],
                           w0_send.at[0, e], w0_recv.at[0, e], device(y, x, le, ce, t)))
        w0.append(send(own, wc.at[l * 2 + c, spot, :, pl.ds(packed, packed)],
                       w0_send.at[1, e], w0_recv.at[1, e], device(y, x, le, ce, pair(ce, t))))
    for copy in w0:
        copy.start()

    swaps = []
    for slot, block in ((0, q), (1, pair(1 - c, q))):
        swaps.append(send(x_ref.at[pl.ds(block * block_rows, block_rows)], xb.at[slot, :, pl.ds(quarter, quarter)],
                          x_send.at[slot], x_recv.at[slot], device(y, x, l, c, q)))
    for copy in own_copies:
        copy.start()
    y_copy = pltpu.make_async_copy(y_ref, yb, y_own)
    y_copy.start()

    def to_both(part, ss, rs, along):
        copies = [send(part(0, slice(None)), part(0, slice(None)), ss.at[i], rs.at[i], along(n)[1])
                  for i, n in ((0, 1), (1, 3))]
        for copy in copies:
            copy.start()
        return copies

    def pass_on(part, ss, rs, along):
        copies = [send(part(back, half), part(back, half), ss.at[i], rs.at[i], along(n)[1])
                  for i, n, back, half in ((2, 1, 3, slice(0, 2)), (3, 3, 1, slice(2, 4)))]
        for copy in copies:
            copy.start()
        return copies

    def part_a(n, half):
        return wc.at[half, b * 4 + lax.rem(a + n, 4)]

    def part_b(n, half):
        return wc.at[half, pl.ds(lax.rem(b + n, 4) * 4, 4)]

    for copy in w0:
        copy.wait_recv()
    for copy in swaps:
        copy.start()
    gathers = []
    for part, ss, rs, along in ((part_a, wa_send, wa_recv, along_a), (part_b, wb_send, wb_recv, along_b)):
        first = to_both(part, ss, rs, along)
        for copy in first:
            copy.wait_recv()
        second = pass_on(part, ss, rs, along)
        if part is part_a:
            for copy in second:
                copy.wait_recv()
        gathers += first + second

    def targets(e, carry):
        le, ce = owner(e)
        row = lax.broadcasted_iota(jnp.int32, (chunk, 1), 0)
        row_b, row_a, row_r = row // 64, (row // 16) % 4, row % 16
        key = (row_b + c * (row_a - row_b)) * 256 + (row_a + c * (row_b - row_a)) * 64 + le * 32 + ce * 16 + row_r
        column = lax.broadcasted_iota(jnp.int32, (chunk, yb.shape[1]), 1)
        choose = jnp.where(column == key, 1.0, 0.0).astype(BF16)
        yt[e] = lax.dot_general(choose, yb[...], (((1,), (1,)), ((), ())),
                                preferred_element_type=F32).astype(BF16)
        return carry

    y_copy.wait()
    lax.fori_loop(0, 4, targets, 0)

    for copy in own_copies:
        copy.wait()
    for copy in second:
        copy.wait_recv()

    def unpack(j, carry):
        for i in range(2 * blocks):
            base = i // blocks * packed + i % blocks * GROUPS
            cols = slice(i * BLOCK, (i + 1) * BLOCK)
            parts = [wc[j, :, :, base + side * third:base + side * third + GROUPS].reshape(chunk, GROUPS)
                     for side in range(3)]
            low, high = kept_places(parts[2], spread)
            wide = [jnp.dot(part, spread, preferred_element_type=F32) for part in parts[:2]]
            wb[j, :, cols] = jnp.where(low, wide[0], jnp.where(high, wide[1], 0.0)).astype(BF16)
            ml[j, :, cols] = jnp.where(low, 1.0, 0.0).astype(BF16)
            mh[j, :, cols] = jnp.where(high, 1.0, 0.0).astype(BF16)
        return carry

    lax.fori_loop(0, 4, unpack, 0)
    swaps[0].wait_recv()

    def partial_copy(e, slot):
        return send(pb.at[e, slot], pr.at[e, 1 - slot], p_send.at[e, slot], p_recv.at[e, 1 - slot],
                    device(y, x, l, c, u))

    def partials(k, carry):
        e = 3 - k
        le, ce = owner(e)
        rows = wb[le * 2 + ce]
        for slot in range(2):
            if slot == 1:
                @pl.when(k == 0)
                def _():
                    swaps[1].wait_recv()
            part = lax.dot_general(rows, xb[slot], (((1,), (1,)), ((), ())), preferred_element_type=F32)
            if slot == 0:
                part = part - yt[e].astype(F32)
            ptf[e, slot] = part
            pb[e, slot] = part.astype(BF16)
            partial_copy(e, slot).start()
        return carry

    lax.fori_loop(0, 4, partials, 0)

    def spread_out(e, i):
        cols = pl.ds(i * piece, piece)

        def one(n, carry):
            spot, to = across(n)
            send(gb.at[e, spot, :, cols], ar.at[e, n - 1, :, cols], a_send.at[e, i], a_recv.at[e, i], to).start()
            return carry

        lax.fori_loop(1, 16, one, 0)

    def all_of(e, i, sem):
        landed = ar.at[e, :, :, pl.ds(i * piece, piece)]
        return pltpu.make_async_copy(landed, landed, sem.at[e, i])

    def f_copy(e, slot):
        le, ce = owner(e)
        return send(zs.at[e, :, pl.ds(slot * half_width, half_width)], fr.at[slot, e],
                    f_send.at[slot, e], f_recv.at[slot, e], device(y, x, le, ce, q if slot else t))

    def gradient(e):
        for slot in range(2):
            partial_copy(e, 1 - slot).wait_recv()
            total = ptf[e, slot] + pr[e, slot].astype(F32)
            sb[:, slot * block_rows:(slot + 1) * block_rows] = (total * scale).astype(BF16)
        le, ce = owner(e)
        j = le * 2 + ce
        for i in reversed(range(PIECES)):
            wide = slice(i * 2 * piece, (i + 1) * 2 * piece)
            rows = xb[:, :, wide].reshape(2 * block_rows, 2 * piece)
            term = jnp.dot(sb[...], rows, preferred_element_type=F32).astype(BF16)
            kept = []
            for n in range(2 * piece // BLOCK):
                cols = slice(n * BLOCK, (n + 1) * BLOCK)
                spot = slice(i * 2 * piece + n * BLOCK, i * 2 * piece + (n + 1) * BLOCK)
                for place in (ml, mh):
                    kept.append(jnp.dot(term[:, cols] * place[j, :, spot], squeeze, preferred_element_type=F32))
            gb[e, :, :, i * piece:(i + 1) * piece] = (
                jnp.concatenate(kept, axis=1).astype(BF16).reshape(16, 16, piece))
            spread_out(e, i)

    def reduce(e):
        for i in reversed(range(PIECES)):
            cols = slice(i * piece, (i + 1) * piece)
            all_of(e, i, a_recv).wait()
            total = gb[e, b * 4 + a, :, cols].astype(F32)
            for n in range(15):
                total = total + ar[e, n, :, cols].astype(F32)
            zs[e, :, cols] = total
            if i * piece == half_width:
                f_copy(e, 1).start()

        @pl.when(e > 0)
        def _():
            f_copy(e, 0).start()

    def steps(k, carry):
        @pl.when(k < 4)
        def _():
            gradient(3 - k)

        @pl.when(k >= 1)
        def _():
            reduce(4 - k)

        return carry

    lax.fori_loop(0, 5, steps, 0)

    total = zs[0, :, 0:half_width]
    for e in range(4):
        if e:
            f_copy(jnp.int32(e), 0).wait_recv()
            total = total + fr[0, e]
        f_copy(jnp.int32(e), 1).wait_recv()
        total = total + fr[1, e]
    for i in range(blocks):
        low, high = kept_places(own[:, 2 * third + i * GROUPS:2 * third + (i + 1) * GROUPS], spread)
        wide = [spread_exactly(total[:, n * GROUPS:(n + 1) * GROUPS], spread) for n in (2 * i, 2 * i + 1)]
        o_ref[:, i * BLOCK:(i + 1) * BLOCK] = jnp.where(low, wide[0], jnp.where(high, wide[1], 0.0))

    for copy in w0 + swaps + gathers:
        copy.wait_send()

    def drain(e, carry):
        for slot in range(2):
            partial_copy(e, slot).wait_send()
        for i in range(PIECES):
            all_of(e, i, a_send).wait()
        f_copy(e, 1).wait_send()

        @pl.when(e > 0)
        def _():
            f_copy(e, 0).wait_send()

        return carry

    lax.fori_loop(0, 4, drain, 0)


def body(teacher_inputs, teacher_keys, w_key, mask_key):
    rows, quarter = teacher_inputs.shape
    block_rows, keys = teacher_keys.shape
    groups = lax.axis_size("teacher") * lax.axis_size("dp")
    scale = 1.0 / math.sqrt(rows * groups)
    width = 2 * quarter
    dma = pltpu.SemaphoreType.DMA
    vmem = pl.BlockSpec(memory_space=pltpu.VMEM)
    return pl.pallas_call(
        functools.partial(kernel, scale),
        out_shape=jax.ShapeDtypeStruct((16, quarter), F32),
        in_specs=[pl.BlockSpec(memory_space=pl.ANY), pl.BlockSpec(memory_space=pl.ANY), vmem, vmem],
        out_specs=vmem,
        scratch_shapes=[
            pltpu.VMEM((2, block_rows, width), BF16),
            pltpu.VMEM((block_rows, keys), BF16),
            pltpu.VMEM((4, 16, 16, 3 * width // 4), BF16),
            pltpu.VMEM((4, keys // 4, width), BF16),
            pltpu.VMEM((4, keys // 4, width), BF16),
            pltpu.VMEM((4, keys // 4, width), BF16),
            pltpu.VMEM((4, keys // 4, block_rows), BF16),
            pltpu.VMEM((4, 2, keys // 4, block_rows), F32),
            pltpu.VMEM((4, 2, keys // 4, block_rows), BF16),
            pltpu.VMEM((4, 2, keys // 4, block_rows), BF16),
            pltpu.VMEM((keys // 4, 2 * block_rows), BF16),
            pltpu.VMEM((4, 16, 16, quarter), BF16),
            pltpu.VMEM((4, 15, 16, quarter), BF16),
            pltpu.VMEM((4, 16, quarter), F32),
            pltpu.VMEM((2, 4, 16, quarter // 2), F32),
            pltpu.VMEM((16, 3 * quarter // 4), BF16),
            dma((2,)), dma((2,)), dma((2,)), dma(()),
            dma((2, 4)), dma((2, 4)),
            dma((4,)), dma((4,)), dma((4,)), dma((4,)),
            dma((4, 2)), dma((4, 2)),
            dma((4, PIECES)), dma((4, PIECES)),
            dma((2, 4)), dma((2, 4)),
        ],
        compiler_params=pltpu.CompilerParams(
            collective_id=0, has_side_effects=True, vmem_limit_bytes=60 * 2**20),
    )(teacher_inputs, teacher_keys, w_key, mask_key)


def solution(mesh):
    placed = (
        P(("teacher", "dp"), "tensor"),
        P(("teacher", "dp", "tensor"), None),
        P(("teacher", "dp"), "tensor"),
        P(("teacher", "dp"), "tensor"),
    )
    return jax.shard_map(
        body, mesh=mesh, in_specs=placed, out_specs=P(("teacher", "dp"), "tensor"), check_vma=False
    )
```

```python
import functools
import math

import jax
import jax.numpy as jnp
from jax import lax
from jax.experimental import pallas as pl
from jax.experimental.pallas import tpu as pltpu
from jax.sharding import PartitionSpec as P

MESH = pl.DeviceIdType.MESH
F32 = jnp.float32
BF16 = jnp.bfloat16
GROUPS = 128
BLOCK = 4 * GROUPS
PIECES = 2


def pair(core, t):
    return (1 - core) * (t + 1 - 2 * lax.rem(t, 2)) + core * (3 - t)


def device(y, x, l, c, t):
    return {"teacher": y, "dp": x * 4 + l * 2 + c, "tensor": t}


def spread_matrix():
    row = lax.broadcasted_iota(jnp.int32, (GROUPS, BLOCK), 0)
    column = lax.broadcasted_iota(jnp.int32, (GROUPS, BLOCK), 1)
    return jnp.where(column // 4 == row, 1.0, 0.0).astype(BF16)


def squeeze_matrix():
    row = lax.broadcasted_iota(jnp.int32, (BLOCK, GROUPS), 0)
    column = lax.broadcasted_iota(jnp.int32, (BLOCK, GROUPS), 1)
    return jnp.where(row // 4 == column, 1.0, 0.0).astype(BF16)


def kept_places(pattern, spread):
    p = jnp.dot(pattern, spread, preferred_element_type=F32)
    place = (lax.broadcasted_iota(jnp.int32, p.shape, 1) % 4).astype(F32)
    upper = jnp.where(p > 2.5, 1.0, 0.0)
    last = jnp.where(p > 4.5, 1.0, 0.0)
    return upper + last == place, p + 1.0 - 2.0 * upper - last == place


def spread_exactly(values, spread):
    total = None
    for _ in range(3):
        part = values.astype(BF16)
        values = values - part.astype(F32)
        wide = jnp.dot(part, spread, preferred_element_type=F32)
        total = wide if total is None else total + wide
    return total


def kernel(scale, x_ref, y_ref, w_ref, mask_ref, o_ref,
           xb, yb, wc, wb, ml, mh, yt, ptf, pb, pr, sb, gb, sr, ar, zs, fr, own,
           x_send, x_recv, x_own, y_own, w0_send, w0_recv, wa_send, wa_recv, wb_send, wb_recv,
           p_send, p_recv, s_send, s_recv, a_send, a_recv, f_send, f_recv):
    y = lax.axis_index("teacher")
    d = lax.axis_index("dp")
    t = lax.axis_index("tensor")
    x = lax.div(d, 4)
    l = lax.rem(lax.div(d, 2), 2)
    c = lax.rem(d, 2)
    a = x + c * (y - x)
    b = y + c * (x - y)
    q = pair(c, t)
    u = pair(1 - c, t)
    block_rows, quarter = xb.shape[1], xb.shape[2] // 2
    blocks = quarter // BLOCK
    third = quarter // 4
    packed = 3 * third
    half_width = quarter // 2
    piece = quarter // PIECES
    chunk = wb.shape[1]

    def along_a(n):
        other = lax.rem(a + n, 4)
        return other, device(y + c * (other - y), x + (1 - c) * (other - x), l, c, t)

    def along_b(n):
        other = lax.rem(b + n, 4)
        return other, device(y + (1 - c) * (other - y), x + c * (other - x), l, c, t)

    def across(n):
        other_a, other_b = lax.rem(a + n % 4, 4), lax.rem(b + n // 4, 4)
        to = device(other_b + c * (other_a - other_b), other_a + c * (other_b - other_a), l, c, t)
        return other_b * 4 + other_a, to

    def owner(e):
        return lax.rem(l + lax.div(e, 2), 2), lax.rem(c + lax.rem(e, 2), 2)

    def send(src, dst, ss, rs, to):
        return pltpu.make_async_remote_copy(
            src_ref=src, dst_ref=dst, send_sem=ss, recv_sem=rs, device_id=to, device_id_type=MESH)

    barrier = pltpu.get_barrier_semaphore()
    friends = [across(n)[1] for n in range(1, 16)] + [device(y, x, l, c, u)]
    for e in range(4):
        le, ce = owner(jnp.int32(e))
        if e:
            friends.append(device(y, x, le, ce, t))
        friends.append(device(y, x, le, ce, q))
        if e % 2:
            friends.append(device(y, x, le, ce, u))
    for friend in friends:
        pl.semaphore_signal(barrier, 1, device_id=friend, device_id_type=MESH)

    own_copies = []
    for slot, block in ((0, t), (1, u)):
        own_copies.append(pltpu.make_async_copy(
            x_ref.at[pl.ds(block * block_rows, block_rows)], xb.at[slot, :, pl.ds(0, quarter)], x_own.at[slot]))
    spread, squeeze = spread_matrix(), squeeze_matrix()
    own[:, 2 * third:] = mask_ref[...].astype(F32).astype(BF16)
    for i in range(blocks):
        low, high = kept_places(own[:, 2 * third + i * GROUPS:2 * third + (i + 1) * GROUPS], spread)
        weights = w_ref[:, i * BLOCK:(i + 1) * BLOCK].astype(F32)
        for side, place in enumerate((low, high)):
            own[:, side * third + i * GROUPS:side * third + (i + 1) * GROUPS] = jnp.dot(
                jnp.where(place, weights, 0.0).astype(BF16), squeeze, preferred_element_type=F32).astype(BF16)
    wc[l * 2 + c, b * 4 + a, :, pl.ds(0, packed)] = own[...]

    pl.semaphore_wait(barrier, len(friends))

    w0 = []
    for e in range(4):
        le, ce = owner(jnp.int32(e))
        spot = (y + ce * (x - y)) * 4 + x + ce * (y - x)
        if e:
            w0.append(send(own, wc.at[l * 2 + c, spot, :, pl.ds(0, packed)],
                           w0_send.at[0, e], w0_recv.at[0, e], device(y, x, le, ce, t)))
        w0.append(send(own, wc.at[l * 2 + c, spot, :, pl.ds(packed, packed)],
                       w0_send.at[1, e], w0_recv.at[1, e], device(y, x, le, ce, pair(ce, t))))
    for copy in w0:
        copy.start()

    swaps = []
    for slot, block in ((0, q), (1, pair(1 - c, q))):
        swaps.append(send(x_ref.at[pl.ds(block * block_rows, block_rows)], xb.at[slot, :, pl.ds(quarter, quarter)],
                          x_send.at[slot], x_recv.at[slot], device(y, x, l, c, q)))
    for copy in own_copies:
        copy.start()
    y_copy = pltpu.make_async_copy(y_ref, yb, y_own)
    y_copy.start()

    def to_both(part, ss, rs, along):
        copies = [send(part(0, slice(None)), part(0, slice(None)), ss.at[i], rs.at[i], along(n)[1])
                  for i, n in ((0, 1), (1, 3))]
        for copy in copies:
            copy.start()
        return copies

    def pass_on(part, ss, rs, along):
        copies = [send(part(back, half), part(back, half), ss.at[i], rs.at[i], along(n)[1])
                  for i, n, back, half in ((2, 1, 3, slice(0, 2)), (3, 3, 1, slice(2, 4)))]
        for copy in copies:
            copy.start()
        return copies

    def part_a(n, half):
        return wc.at[half, b * 4 + lax.rem(a + n, 4)]

    def part_b(n, half):
        return wc.at[half, pl.ds(lax.rem(b + n, 4) * 4, 4)]

    for copy in w0:
        copy.wait_recv()
    for copy in swaps:
        copy.start()
    gathers = []
    for part, ss, rs, along in ((part_a, wa_send, wa_recv, along_a), (part_b, wb_send, wb_recv, along_b)):
        first = to_both(part, ss, rs, along)
        for copy in first:
            copy.wait_recv()
        second = pass_on(part, ss, rs, along)
        if part is part_a:
            for copy in second:
                copy.wait_recv()
        gathers += first + second

    def targets(e, carry):
        le, ce = owner(e)
        row = lax.broadcasted_iota(jnp.int32, (chunk, 1), 0)
        row_b, row_a, row_r = row // 64, (row // 16) % 4, row % 16
        key = (row_b + c * (row_a - row_b)) * 256 + (row_a + c * (row_b - row_a)) * 64 + le * 32 + ce * 16 + row_r
        column = lax.broadcasted_iota(jnp.int32, (chunk, yb.shape[1]), 1)
        choose = jnp.where(column == key, 1.0, 0.0).astype(BF16)
        yt[e] = lax.dot_general(choose, yb[...], (((1,), (1,)), ((), ())),
                                preferred_element_type=F32).astype(BF16)
        return carry

    y_copy.wait()
    lax.fori_loop(0, 4, targets, 0)

    for copy in own_copies:
        copy.wait()
    for copy in second:
        copy.wait_recv()

    def unpack(j, carry):
        for i in range(2 * blocks):
            base = i // blocks * packed + i % blocks * GROUPS
            cols = slice(i * BLOCK, (i + 1) * BLOCK)
            parts = [wc[j, :, :, base + side * third:base + side * third + GROUPS].reshape(chunk, GROUPS)
                     for side in range(3)]
            low, high = kept_places(parts[2], spread)
            wide = [jnp.dot(part, spread, preferred_element_type=F32) for part in parts[:2]]
            wb[j, :, cols] = jnp.where(low, wide[0], jnp.where(high, wide[1], 0.0)).astype(BF16)
            ml[j, :, cols] = jnp.where(low, 1.0, 0.0).astype(BF16)
            mh[j, :, cols] = jnp.where(high, 1.0, 0.0).astype(BF16)
        return carry

    lax.fori_loop(0, 4, unpack, 0)
    swaps[0].wait_recv()

    def partial_copy(e, slot):
        return send(pb.at[e, slot], pr.at[e, 1 - slot], p_send.at[e, slot], p_recv.at[e, 1 - slot],
                    device(y, x, l, c, u))

    def partials(k, carry):
        e = 3 - k
        le, ce = owner(e)
        rows = wb[le * 2 + ce]
        for slot in range(2):
            if slot == 1:
                @pl.when(k == 0)
                def _():
                    swaps[1].wait_recv()
            part = lax.dot_general(rows, xb[slot], (((1,), (1,)), ((), ())), preferred_element_type=F32)
            if slot == 0:
                part = part - yt[e].astype(F32)
            ptf[e, slot] = part
            pb[e, slot] = part.astype(BF16)
            partial_copy(e, slot).start()
        return carry

    lax.fori_loop(0, 4, partials, 0)

    def across_chip(e):
        return send(gb.at[e, :, :, pl.ds(0, piece)], sr.at[lax.div(e, 2)], s_send.at[lax.div(e, 2)],
                    s_recv.at[lax.div(e, 2)], device(y, x, l, 1 - c, t))

    def spread_out(e, i):
        cols = pl.ds(i * piece, piece)

        def one(n, carry):
            spot, to = across(n)
            send(gb.at[e, spot, :, cols], ar.at[e, n - 1, :, cols], a_send.at[e, i], a_recv.at[e, i], to).start()
            return carry

        lax.fori_loop(1, 16, one, 0)

    def all_of(e, i, sem):
        landed = ar.at[e, :, :, pl.ds(i * piece, piece)]
        return pltpu.make_async_copy(landed, landed, sem.at[e, i])

    def f_copy(e, slot):
        le, ce = owner(e)
        return send(zs.at[e, :, pl.ds(slot * half_width, half_width)], fr.at[slot, e],
                    f_send.at[slot, e], f_recv.at[slot, e], device(y, x, le, ce, q if slot else t))

    def gradient(e):
        for slot in range(2):
            partial_copy(e, 1 - slot).wait_recv()
            total = ptf[e, slot] + pr[e, slot].astype(F32)
            sb[:, slot * block_rows:(slot + 1) * block_rows] = (total * scale).astype(BF16)
        le, ce = owner(e)
        j = le * 2 + ce
        for i in reversed(range(PIECES)):
            wide = slice(i * 2 * piece, (i + 1) * 2 * piece)
            rows = xb[:, :, wide].reshape(2 * block_rows, 2 * piece)
            term = jnp.dot(sb[...], rows, preferred_element_type=F32).astype(BF16)
            kept = []
            for n in range(2 * piece // BLOCK):
                cols = slice(n * BLOCK, (n + 1) * BLOCK)
                spot = slice(i * 2 * piece + n * BLOCK, i * 2 * piece + (n + 1) * BLOCK)
                for place in (ml, mh):
                    kept.append(jnp.dot(term[:, cols] * place[j, :, spot], squeeze, preferred_element_type=F32))
            gb[e, :, :, i * piece:(i + 1) * piece] = (
                jnp.concatenate(kept, axis=1).astype(BF16).reshape(16, 16, piece))
            if i:
                spread_out(e, i)

        odd = lax.rem(e, 2)

        @pl.when(odd == 1)
        def _():
            across_chip(e).start()

        @pl.when(odd == 0)
        def _():
            across_chip(e).wait_recv()
            for spot in range(16):
                other = spot % 4 * 4 + spot // 4
                gb[e, spot, :, 0:piece] = (gb[e, spot, :, 0:piece].astype(F32)
                                           + sr[lax.div(e, 2), other].astype(F32)).astype(BF16)
            spread_out(e, 0)

    def reduce_slot(e, i):
        cols = slice(i * piece, (i + 1) * piece)
        all_of(e, i, a_recv).wait()
        total = gb[e, b * 4 + a, :, cols].astype(F32)
        for n in range(15):
            total = total + ar[e, n, :, cols].astype(F32)
        zs[e, :, cols] = total

    def reduce(e):
        reduce_slot(e, 1)
        f_copy(e, 1).start()

        @pl.when(lax.rem(e, 2) == 0)
        def _():
            reduce_slot(e, 0)

        @pl.when(e == 2)
        def _():
            f_copy(e, 0).start()

    def steps(k, carry):
        @pl.when(k < 4)
        def _():
            gradient(3 - k)

        @pl.when(k >= 1)
        def _():
            reduce(4 - k)

        return carry

    lax.fori_loop(0, 5, steps, 0)

    for copy in w0 + swaps + gathers:
        copy.wait_send()

    def drain(e, carry):
        for slot in range(2):
            partial_copy(e, slot).wait_send()
        all_of(e, 1, a_send).wait()

        @pl.when(lax.rem(e, 2) == 1)
        def _():
            across_chip(e).wait_send()

        @pl.when(lax.rem(e, 2) == 0)
        def _():
            all_of(e, 0, a_send).wait()

        @pl.when(e > 0)
        def _():
            f_copy(e, 1).wait_send()

        return carry

    lax.fori_loop(0, 4, drain, 0)
    two = jnp.int32(2)
    f_copy(two, 0).wait_send()
    f_copy(two, 0).wait_recv()
    total = zs[0, :, 0:half_width] + fr[0, 2]
    for e in (3, 2, 1, 0):
        f_copy(jnp.int32(e), 1).wait_recv()
        total = total + fr[1, e]
    for i in range(blocks):
        low, high = kept_places(own[:, 2 * third + i * GROUPS:2 * third + (i + 1) * GROUPS], spread)
        wide = [spread_exactly(total[:, n * GROUPS:(n + 1) * GROUPS], spread) for n in (2 * i, 2 * i + 1)]
        o_ref[:, i * BLOCK:(i + 1) * BLOCK] = jnp.where(low, wide[0], jnp.where(high, wide[1], 0.0))
    f_copy(jnp.int32(0), 1).wait_send()


def body(teacher_inputs, teacher_keys, w_key, mask_key):
    rows, quarter = teacher_inputs.shape
    block_rows, keys = teacher_keys.shape
    groups = lax.axis_size("teacher") * lax.axis_size("dp")
    scale = 1.0 / math.sqrt(rows * groups)
    width = 2 * quarter
    dma = pltpu.SemaphoreType.DMA
    vmem = pl.BlockSpec(memory_space=pltpu.VMEM)
    return pl.pallas_call(
        functools.partial(kernel, scale),
        out_shape=jax.ShapeDtypeStruct((16, quarter), F32),
        in_specs=[pl.BlockSpec(memory_space=pl.ANY), pl.BlockSpec(memory_space=pl.ANY), vmem, vmem],
        out_specs=vmem,
        scratch_shapes=[
            pltpu.VMEM((2, block_rows, width), BF16),
            pltpu.VMEM((block_rows, keys), BF16),
            pltpu.VMEM((4, 16, 16, 3 * width // 4), BF16),
            pltpu.VMEM((4, keys // 4, width), BF16),
            pltpu.VMEM((4, keys // 4, width), BF16),
            pltpu.VMEM((4, keys // 4, width), BF16),
            pltpu.VMEM((4, keys // 4, block_rows), BF16),
            pltpu.VMEM((4, 2, keys // 4, block_rows), F32),
            pltpu.VMEM((4, 2, keys // 4, block_rows), BF16),
            pltpu.VMEM((4, 2, keys // 4, block_rows), BF16),
            pltpu.VMEM((keys // 4, 2 * block_rows), BF16),
            pltpu.VMEM((4, 16, 16, quarter), BF16),
            pltpu.VMEM((2, 16, 16, quarter // 2), BF16),
            pltpu.VMEM((4, 15, 16, quarter), BF16),
            pltpu.VMEM((4, 16, quarter), F32),
            pltpu.VMEM((2, 4, 16, quarter // 2), F32),
            pltpu.VMEM((16, 3 * quarter // 4), BF16),
            dma((2,)), dma((2,)), dma((2,)), dma(()),
            dma((2, 4)), dma((2, 4)),
            dma((4,)), dma((4,)), dma((4,)), dma((4,)),
            dma((4, 2)), dma((4, 2)),
            dma((2,)), dma((2,)),
            dma((4, PIECES)), dma((4, PIECES)),
            dma((2, 4)), dma((2, 4)),
        ],
        compiler_params=pltpu.CompilerParams(
            collective_id=0, has_side_effects=True, vmem_limit_bytes=60 * 2**20),
    )(teacher_inputs, teacher_keys, w_key, mask_key)


def solution(mesh):
    placed = (
        P(("teacher", "dp"), "tensor"),
        P(("teacher", "dp", "tensor"), None),
        P(("teacher", "dp"), "tensor"),
        P(("teacher", "dp"), "tensor"),
    )
    return jax.shard_map(
        body, mesh=mesh, in_specs=placed, out_specs=P(("teacher", "dp"), "tensor"), check_vma=False
    )
```

```python
import functools
import math

import jax
import jax.numpy as jnp
from jax import lax
from jax.experimental import pallas as pl
from jax.experimental.pallas import tpu as pltpu
from jax.sharding import PartitionSpec as P

MESH = pl.DeviceIdType.MESH
F32 = jnp.float32
BF16 = jnp.bfloat16
GROUPS = 128
BLOCK = 4 * GROUPS
PIECES = 2


def pair(core, t):
    return (1 - core) * (t + 1 - 2 * lax.rem(t, 2)) + core * (3 - t)


def device(y, x, l, c, t):
    return {"teacher": y, "dp": x * 4 + l * 2 + c, "tensor": t}


def spread_matrix():
    row = lax.broadcasted_iota(jnp.int32, (GROUPS, BLOCK), 0)
    column = lax.broadcasted_iota(jnp.int32, (GROUPS, BLOCK), 1)
    return jnp.where(column // 4 == row, 1.0, 0.0).astype(BF16)


def squeeze_matrix():
    row = lax.broadcasted_iota(jnp.int32, (BLOCK, GROUPS), 0)
    column = lax.broadcasted_iota(jnp.int32, (BLOCK, GROUPS), 1)
    return jnp.where(row // 4 == column, 1.0, 0.0).astype(BF16)


def kept_places(pattern, spread):
    p = jnp.dot(pattern, spread, preferred_element_type=F32)
    place = (lax.broadcasted_iota(jnp.int32, p.shape, 1) % 4).astype(F32)
    upper = jnp.where(p > 2.5, 1.0, 0.0)
    last = jnp.where(p > 4.5, 1.0, 0.0)
    return upper + last == place, p + 1.0 - 2.0 * upper - last == place


def spread_exactly(values, spread):
    total = None
    for _ in range(3):
        part = values.astype(BF16)
        values = values - part.astype(F32)
        wide = jnp.dot(part, spread, preferred_element_type=F32)
        total = wide if total is None else total + wide
    return total


def kernel(scale, x_ref, y_ref, w_ref, mask_ref, o_ref,
           xb, yb, wc, wb, ml, mh, yt, ptf, pb, pr, sb, gb, sr, ar, zs, fr, own,
           x_send, x_recv, x_own, y_own, w0_send, w0_recv, wa_send, wa_recv, wb_send, wb_recv,
           p_send, p_recv, s_send, s_recv, a_send, a_recv, f_send, f_recv):
    y = lax.axis_index("teacher")
    d = lax.axis_index("dp")
    t = lax.axis_index("tensor")
    x = lax.div(d, 4)
    l = lax.rem(lax.div(d, 2), 2)
    c = lax.rem(d, 2)
    a = x + c * (y - x)
    b = y + c * (x - y)
    q = pair(c, t)
    u = pair(1 - c, t)
    block_rows, quarter = xb.shape[1], xb.shape[2] // 2
    blocks = quarter // BLOCK
    third = quarter // 4
    packed = 3 * third
    half_width = quarter // 2
    piece = quarter // PIECES
    chunk = wb.shape[1]

    def along_a(n):
        other = lax.rem(a + n, 4)
        return other, device(y + c * (other - y), x + (1 - c) * (other - x), l, c, t)

    def along_b(n):
        other = lax.rem(b + n, 4)
        return other, device(y + (1 - c) * (other - y), x + c * (other - x), l, c, t)

    def across(n):
        other_a, other_b = lax.rem(a + n % 4, 4), lax.rem(b + n // 4, 4)
        to = device(other_b + c * (other_a - other_b), other_a + c * (other_b - other_a), l, c, t)
        return other_b * 4 + other_a, to

    def owner(e):
        return lax.rem(l + lax.div(e, 2), 2), lax.rem(c + lax.rem(e, 2), 2)

    def send(src, dst, ss, rs, to):
        return pltpu.make_async_remote_copy(
            src_ref=src, dst_ref=dst, send_sem=ss, recv_sem=rs, device_id=to, device_id_type=MESH)

    barrier = pltpu.get_barrier_semaphore()
    friends = [across(n)[1] for n in range(1, 16)] + [device(y, x, l, c, u)]
    for e in range(4):
        le, ce = owner(jnp.int32(e))
        if e:
            friends.append(device(y, x, le, ce, t))
        friends.append(device(y, x, le, ce, q))
        if e % 2:
            friends.append(device(y, x, le, ce, u))
    for friend in friends:
        pl.semaphore_signal(barrier, 1, device_id=friend, device_id_type=MESH)

    own_copies = []
    for slot, block in ((0, t), (1, u)):
        own_copies.append(pltpu.make_async_copy(
            x_ref.at[pl.ds(block * block_rows, block_rows)], xb.at[slot, :, pl.ds(0, quarter)], x_own.at[slot]))
    spread, squeeze = spread_matrix(), squeeze_matrix()
    own[:, 2 * third:] = mask_ref[...].astype(F32).astype(BF16)
    for i in range(blocks):
        low, high = kept_places(own[:, 2 * third + i * GROUPS:2 * third + (i + 1) * GROUPS], spread)
        weights = w_ref[:, i * BLOCK:(i + 1) * BLOCK].astype(F32)
        for side, place in enumerate((low, high)):
            own[:, side * third + i * GROUPS:side * third + (i + 1) * GROUPS] = jnp.dot(
                jnp.where(place, weights, 0.0).astype(BF16), squeeze, preferred_element_type=F32).astype(BF16)
    wc[l * 2 + c, b * 4 + a, :, pl.ds(0, packed)] = own[...]

    pl.semaphore_wait(barrier, len(friends))

    w0 = []
    for e in range(4):
        le, ce = owner(jnp.int32(e))
        spot = (y + ce * (x - y)) * 4 + x + ce * (y - x)
        if e:
            w0.append(send(own, wc.at[l * 2 + c, spot, :, pl.ds(0, packed)],
                           w0_send.at[0, e], w0_recv.at[0, e], device(y, x, le, ce, t)))
        w0.append(send(own, wc.at[l * 2 + c, spot, :, pl.ds(packed, packed)],
                       w0_send.at[1, e], w0_recv.at[1, e], device(y, x, le, ce, pair(ce, t))))
    for copy in w0:
        copy.start()

    swaps = []
    for slot, block in ((0, q), (1, pair(1 - c, q))):
        swaps.append(send(x_ref.at[pl.ds(block * block_rows, block_rows)], xb.at[slot, :, pl.ds(quarter, quarter)],
                          x_send.at[slot], x_recv.at[slot], device(y, x, l, c, q)))
    for copy in own_copies:
        copy.start()
    y_copy = pltpu.make_async_copy(y_ref, yb, y_own)
    y_copy.start()

    def to_both(part, ss, rs, along):
        copies = [send(part(0, slice(None)), part(0, slice(None)), ss.at[i], rs.at[i], along(n)[1])
                  for i, n in ((0, 1), (1, 3))]
        for copy in copies:
            copy.start()
        return copies

    def pass_on(part, ss, rs, along):
        copies = [send(part(back, half), part(back, half), ss.at[i], rs.at[i], along(n)[1])
                  for i, n, back, half in ((2, 1, 3, slice(0, 2)), (3, 3, 1, slice(2, 4)))]
        for copy in copies:
            copy.start()
        return copies

    def part_a(n, half):
        return wc.at[half, b * 4 + lax.rem(a + n, 4)]

    def part_b(n, half):
        return wc.at[half, pl.ds(lax.rem(b + n, 4) * 4, 4)]

    for copy in w0:
        copy.wait_recv()
    for copy in swaps:
        copy.start()
    gathers = []
    for part, ss, rs, along in ((part_a, wa_send, wa_recv, along_a), (part_b, wb_send, wb_recv, along_b)):
        first = to_both(part, ss, rs, along)
        for copy in first:
            copy.wait_recv()
        second = pass_on(part, ss, rs, along)
        if part is part_a:
            for copy in second:
                copy.wait_recv()
        gathers += first + second

    def targets(e, carry):
        le, ce = owner(e)
        row = lax.broadcasted_iota(jnp.int32, (chunk, 1), 0)
        row_b, row_a, row_r = row // 64, (row // 16) % 4, row % 16
        key = (row_b + c * (row_a - row_b)) * 256 + (row_a + c * (row_b - row_a)) * 64 + le * 32 + ce * 16 + row_r
        column = lax.broadcasted_iota(jnp.int32, (chunk, yb.shape[1]), 1)
        choose = jnp.where(column == key, 1.0, 0.0).astype(BF16)
        yt[e] = lax.dot_general(choose, yb[...], (((1,), (1,)), ((), ())),
                                preferred_element_type=F32).astype(BF16)
        return carry

    y_copy.wait()
    lax.fori_loop(0, 4, targets, 0)

    for copy in own_copies:
        copy.wait()
    for copy in second:
        copy.wait_recv()

    def unpack(j, carry):
        for i in range(2 * blocks):
            base = i // blocks * packed + i % blocks * GROUPS
            cols = slice(i * BLOCK, (i + 1) * BLOCK)
            parts = [wc[j, :, :, base + side * third:base + side * third + GROUPS].reshape(chunk, GROUPS)
                     for side in range(3)]
            low, high = kept_places(parts[2], spread)
            wide = [jnp.dot(part, spread, preferred_element_type=F32) for part in parts[:2]]
            wb[j, :, cols] = jnp.where(low, wide[0], jnp.where(high, wide[1], 0.0)).astype(BF16)
            ml[j, :, cols] = jnp.where(low, 1.0, 0.0).astype(BF16)
            mh[j, :, cols] = jnp.where(high, 1.0, 0.0).astype(BF16)
        return carry

    lax.fori_loop(0, 4, unpack, 0)
    swaps[0].wait_recv()

    def partial_copy(e, slot):
        return send(pb.at[e, slot], pr.at[e, 1 - slot], p_send.at[e, slot], p_recv.at[e, 1 - slot],
                    device(y, x, l, c, u))

    def partials(k, carry):
        e = 3 - k
        le, ce = owner(e)
        rows = wb[le * 2 + ce]
        for slot in range(2):
            if slot == 1:
                @pl.when(k == 0)
                def _():
                    swaps[1].wait_recv()
            part = lax.dot_general(rows, xb[slot], (((1,), (1,)), ((), ())), preferred_element_type=F32)
            if slot == 0:
                part = part - yt[e].astype(F32)
            ptf[e, slot] = part
            pb[e, slot] = part.astype(BF16)

            @pl.when(k < 2)
            def _():
                partial_copy(e, slot).start()

        return carry

    lax.fori_loop(0, 4, partials, 0)

    def across_chip(e):
        return send(gb.at[e, :, :, pl.ds(0, piece)], sr.at[lax.div(e, 2)], s_send.at[lax.div(e, 2)],
                    s_recv.at[lax.div(e, 2)], device(y, x, l, 1 - c, t))

    def spread_out(e, i):
        cols = pl.ds(i * piece, piece)

        def one(n, carry):
            spot, to = across(n)
            send(gb.at[e, spot, :, cols], ar.at[e, n - 1, :, cols], a_send.at[e, i], a_recv.at[e, i], to).start()
            return carry

        lax.fori_loop(1, 16, one, 0)

    def all_of(e, i, sem):
        landed = ar.at[e, :, :, pl.ds(i * piece, piece)]
        return pltpu.make_async_copy(landed, landed, sem.at[e, i])

    def f_copy(e, slot):
        le, ce = owner(e)
        return send(zs.at[e, :, pl.ds(slot * half_width, half_width)], fr.at[slot, e],
                    f_send.at[slot, e], f_recv.at[slot, e], device(y, x, le, ce, q if slot else t))

    def gradient(e):
        for slot in range(2):
            partial_copy(e, 1 - slot).wait_recv()
            total = ptf[e, slot] + pr[e, slot].astype(F32)
            sb[:, slot * block_rows:(slot + 1) * block_rows] = (total * scale).astype(BF16)

        @pl.when(e >= 2)
        def _():
            for slot in range(2):
                partial_copy(e - 2, slot).start()

        le, ce = owner(e)
        j = le * 2 + ce
        for i in reversed(range(PIECES)):
            wide = slice(i * 2 * piece, (i + 1) * 2 * piece)
            rows = xb[:, :, wide].reshape(2 * block_rows, 2 * piece)
            term = jnp.dot(sb[...], rows, preferred_element_type=F32).astype(BF16)
            kept = []
            for n in range(2 * piece // BLOCK):
                cols = slice(n * BLOCK, (n + 1) * BLOCK)
                spot = slice(i * 2 * piece + n * BLOCK, i * 2 * piece + (n + 1) * BLOCK)
                for place in (ml, mh):
                    kept.append(jnp.dot(term[:, cols] * place[j, :, spot], squeeze, preferred_element_type=F32))
            gb[e, :, :, i * piece:(i + 1) * piece] = (
                jnp.concatenate(kept, axis=1).astype(BF16).reshape(16, 16, piece))
            if i:
                spread_out(e, i)

        odd = lax.rem(e, 2)

        @pl.when(odd == 1)
        def _():
            across_chip(e).start()

        @pl.when(odd == 0)
        def _():
            across_chip(e).wait_recv()
            for spot in range(16):
                other = spot % 4 * 4 + spot // 4
                gb[e, spot, :, 0:piece] = (gb[e, spot, :, 0:piece].astype(F32)
                                           + sr[lax.div(e, 2), other].astype(F32)).astype(BF16)
            spread_out(e, 0)

    def reduce_slot(e, i):
        cols = slice(i * piece, (i + 1) * piece)
        all_of(e, i, a_recv).wait()
        total = gb[e, b * 4 + a, :, cols].astype(F32)
        for n in range(15):
            total = total + ar[e, n, :, cols].astype(F32)
        zs[e, :, cols] = total

    def reduce(e):
        reduce_slot(e, 1)
        f_copy(e, 1).start()

        @pl.when(lax.rem(e, 2) == 0)
        def _():
            reduce_slot(e, 0)

        @pl.when(e == 2)
        def _():
            f_copy(e, 0).start()

    def steps(k, carry):
        @pl.when(k < 4)
        def _():
            gradient(3 - k)

        @pl.when(k >= 2)
        def _():
            reduce(5 - k)

        return carry

    lax.fori_loop(0, 6, steps, 0)

    for copy in w0 + swaps + gathers:
        copy.wait_send()

    def drain(e, carry):
        for slot in range(2):
            partial_copy(e, slot).wait_send()
        all_of(e, 1, a_send).wait()

        @pl.when(lax.rem(e, 2) == 1)
        def _():
            across_chip(e).wait_send()

        @pl.when(lax.rem(e, 2) == 0)
        def _():
            all_of(e, 0, a_send).wait()

        @pl.when(e > 0)
        def _():
            f_copy(e, 1).wait_send()

        return carry

    lax.fori_loop(0, 4, drain, 0)
    two = jnp.int32(2)
    f_copy(two, 0).wait_send()
    f_copy(two, 0).wait_recv()
    total = zs[0, :, 0:half_width] + fr[0, 2]
    for e in (3, 2, 1, 0):
        f_copy(jnp.int32(e), 1).wait_recv()
        total = total + fr[1, e]
    for i in range(blocks):
        low, high = kept_places(own[:, 2 * third + i * GROUPS:2 * third + (i + 1) * GROUPS], spread)
        wide = [spread_exactly(total[:, n * GROUPS:(n + 1) * GROUPS], spread) for n in (2 * i, 2 * i + 1)]
        o_ref[:, i * BLOCK:(i + 1) * BLOCK] = jnp.where(low, wide[0], jnp.where(high, wide[1], 0.0))
    f_copy(jnp.int32(0), 1).wait_send()


def body(teacher_inputs, teacher_keys, w_key, mask_key):
    rows, quarter = teacher_inputs.shape
    block_rows, keys = teacher_keys.shape
    groups = lax.axis_size("teacher") * lax.axis_size("dp")
    scale = 1.0 / math.sqrt(rows * groups)
    width = 2 * quarter
    dma = pltpu.SemaphoreType.DMA
    vmem = pl.BlockSpec(memory_space=pltpu.VMEM)
    return pl.pallas_call(
        functools.partial(kernel, scale),
        out_shape=jax.ShapeDtypeStruct((16, quarter), F32),
        in_specs=[pl.BlockSpec(memory_space=pl.ANY), pl.BlockSpec(memory_space=pl.ANY), vmem, vmem],
        out_specs=vmem,
        scratch_shapes=[
            pltpu.VMEM((2, block_rows, width), BF16),
            pltpu.VMEM((block_rows, keys), BF16),
            pltpu.VMEM((4, 16, 16, 3 * width // 4), BF16),
            pltpu.VMEM((4, keys // 4, width), BF16),
            pltpu.VMEM((4, keys // 4, width), BF16),
            pltpu.VMEM((4, keys // 4, width), BF16),
            pltpu.VMEM((4, keys // 4, block_rows), BF16),
            pltpu.VMEM((4, 2, keys // 4, block_rows), F32),
            pltpu.VMEM((4, 2, keys // 4, block_rows), BF16),
            pltpu.VMEM((4, 2, keys // 4, block_rows), BF16),
            pltpu.VMEM((keys // 4, 2 * block_rows), BF16),
            pltpu.VMEM((4, 16, 16, quarter), BF16),
            pltpu.VMEM((2, 16, 16, quarter // 2), BF16),
            pltpu.VMEM((4, 15, 16, quarter), BF16),
            pltpu.VMEM((4, 16, quarter), F32),
            pltpu.VMEM((2, 4, 16, quarter // 2), F32),
            pltpu.VMEM((16, 3 * quarter // 4), BF16),
            dma((2,)), dma((2,)), dma((2,)), dma(()),
            dma((2, 4)), dma((2, 4)),
            dma((4,)), dma((4,)), dma((4,)), dma((4,)),
            dma((4, 2)), dma((4, 2)),
            dma((2,)), dma((2,)),
            dma((4, PIECES)), dma((4, PIECES)),
            dma((2, 4)), dma((2, 4)),
        ],
        compiler_params=pltpu.CompilerParams(
            collective_id=0, has_side_effects=True, vmem_limit_bytes=60 * 2**20),
    )(teacher_inputs, teacher_keys, w_key, mask_key)


def solution(mesh):
    placed = (
        P(("teacher", "dp"), "tensor"),
        P(("teacher", "dp", "tensor"), None),
        P(("teacher", "dp"), "tensor"),
        P(("teacher", "dp"), "tensor"),
    )
    return jax.shard_map(
        body, mesh=mesh, in_specs=placed, out_specs=P(("teacher", "dp"), "tensor"), check_vma=False
    )
```
